32 devices in a mesh: dp: 4 (over y, core), expert: 8 (over z, x).
Axes of the slice: x: 2, y: 2, z: 4, core: 2. Of those that a mesh axis runs over, the one named last changes fastest.
Arguments:
- tokens: bfloat16 [2048, 2048], P(('dp', 'expert')), may hold values from -6 to 6
- expert_ids: int32 [2048, 8], P(('dp', 'expert')), may hold values from 0 to 127, all different within a row; in each aligned block of 64 rows (0 to 63, 64 to 127, ...) at most 8 rows name the same one
- gate_weight: bfloat16 [8, 2048, 768], P('expert', 'dp'), may hold values from -0.125 to 0.125
- up_weight: bfloat16 [8, 2048, 768], P('expert', 'dp'), may hold values from -0.125 to 0.125
- down_weight: bfloat16 [8, 768, 2048], P('expert', None, 'dp'), may hold values from -6 to 6
Outputs:
- factor: float32 [8, 768, 768], P('expert', 'dp')
- whitened: float32 [8, 768, 2048], P('expert', None, 'dp')
The draws below stay inside these ranges and needn't reach their ends.
Inputs may be any that keep to these rules, and one draw needn't show every extreme that they name: `expert_ids`: each row names 8 different experts. Among the rows of one device (aligned blocks of 64 rows) no expert is named more than 8 times, a bound that some block reaches. Only experts below 8 enter the outputs.
All inputs are finite; a program needn't handle non-finite values.
Results may differ from the reference program's by a relative error of at most 0.0035.
Values may be sent and summed in bfloat16 or wider, within the bound.
No kernel may reach another device: no remote copies, remote signals or barrier semaphores. Data moves between devices by JAX's collectives and lax.ppermute only.
A program may use at most 128 MiB of HBM per device.

```python
import math
import jax
import jax.numpy as jnp
import numpy as np
from jax import lax

D = 2048
FW = 768
EXPERTS_ALL = 128
TOP = 8
TOK_DEV = 64
CAP = 8
EXPERTS = 8
TOKENS = 2048
SLOTS_DEV = 64
N_DP = 4
N_EXPERT = 8


def levels(key, shape, shards, low, top_value):
    level, own = 1.0, jax.random.fold_in(key, 6)
    for axis_at, blocks in shards:
        heights = jnp.exp(jax.random.uniform(jax.random.fold_in(own, axis_at), (blocks,), jnp.float32, low / len(shards), top_value / len(shards)))
        level = level * jnp.repeat(heights, shape[axis_at] // blocks).reshape([-1 if axis == axis_at else 1 for axis in range(len(shape))])
    return level


def shared_out(own_key, own, number, rows, amount, top, limit, skew):
    ranking = jax.random.permutation(own_key, amount)
    packed, usual = load_shares(amount, rows * top, limit, skew, True), load_shares(amount, rows * top, limit, skew, False)
    places = jnp.arange(amount)

    def named(sizes, rotation):
        used = int((sizes > 0).sum())
        fixed = max(1, used // 4)
        shifted = fixed + (places - fixed + rotation * (used - fixed)) % max(1, amount - fixed)
        return jnp.zeros((amount,), jnp.int32).at[ranking[jnp.where(places < fixed, places, shifted)]].set(jnp.asarray(sizes, jnp.int32))

    sizes = jnp.where(number % 4 == 0, named(packed, number // 4), named(usual, number - number // 4 - 1))
    mixed = jax.random.permutation(jax.random.fold_in(own, 3), amount)
    source_of, receiver = mixed[0:amount // 2 * 2:2], mixed[1:amount // 2 * 2:2]
    room = jnp.minimum(sizes[source_of] - 1, limit - sizes[receiver]) // 2
    room = jnp.where((source_of == ranking[0]) | (receiver == ranking[0]) | (sizes[receiver] == 0), 0, jnp.maximum(room, 0))
    shifted = jax.random.randint(jax.random.fold_in(own, 4), (amount // 2,), 0, 1 << 20) % (room + 1)
    sizes = sizes.at[source_of].add(-shifted).at[receiver].add(shifted)
    members = jnp.searchsorted(jnp.cumsum(sizes), jnp.arange(rows * top), side="right").astype(jnp.int32)
    listing = members.reshape(top, rows).T
    listing = listing[jax.random.permutation(jax.random.fold_in(own, 1), rows)]
    rotation = jax.random.randint(jax.random.fold_in(own, 2), (rows, 1), 0, top)
    return jnp.take_along_axis(listing, (jnp.arange(top)[None, :] + rotation) % top, axis=1)


def load_shares(count, total, reach, skew, full):
    weights = [(1 << 20) // math.isqrt(standing ** skew) + 1 for standing in range(1, count + 1)]
    largest = reach if full else min(reach, max(-(-total // count), total * weights[0] // sum(weights)))
    least = 1 if total - largest >= count - 1 else 0
    given, surplus = [largest] + [least] * (count - 1), total - largest - least * (count - 1)
    while surplus > 0:
        candidates = [i for i in range(1, count) if given[i] < largest] or [i for i in range(1, count) if given[i] < reach]
        pool, budget = sum([weights[i] for i in candidates]), surplus
        for i in candidates:
            more = min(reach - given[i], max(1, budget * weights[i] // pool), surplus)
            given[i] = given[i] + more
            surplus = surplus - more
    return np.array(given)


def scatter_about(stream_key, dims, scale, limit, pieces=(), kind=jnp.bfloat16):
    level = levels(stream_key, dims, pieces, -0.22, 0.18) if pieces else 1.0
    values = jax.random.normal(stream_key, dims, jnp.float32) * scale * level
    return jnp.minimum(jnp.maximum(values, -limit), limit).astype(kind)


def setup_inputs(seed: int = 0) -> dict:
    key_list = jax.random.split(jax.random.key(seed), 6)
    tokens = scatter_about(key_list[0], (TOKENS, D), 1.0, 6.0, ((0, 32),))
    expert_ids_keys = jax.random.split(jax.random.fold_in(key_list[1], 1), TOKENS // TOK_DEV)
    expert_ids_turns = jax.random.permutation(jax.random.fold_in(key_list[1], 3), TOKENS // TOK_DEV)
    expert_ids = jax.vmap(lambda own, number: shared_out(jax.random.fold_in(key_list[1], 2), own, number, TOK_DEV, EXPERTS_ALL, TOP, CAP, 2))(expert_ids_keys, expert_ids_turns).reshape((TOKENS, TOP))
    gate_weight = scatter_about(key_list[2], (EXPERTS, D, FW), D ** -0.5, 0.125, ((0, 8), (1, 4)))
    up_weight = scatter_about(key_list[3], (EXPERTS, D, FW), D ** -0.5, 0.125, ((0, 8), (1, 4)))
    down_weight = scatter_about(key_list[4], (EXPERTS, FW, D), 1.0, 6.0, ((0, 8), (2, 4)))
    return dict(tokens=tokens, expert_ids=expert_ids, gate_weight=gate_weight, up_weight=up_weight, down_weight=down_weight)


damping = 0.02

def reference(tokens, expert_ids, gate_weight, up_weight, down_weight):
    slot_count = N_DP * N_EXPERT * CAP
    identity = jnp.eye(FW, dtype=jnp.float32)

    def per_expert(expert):
        member = jnp.any(expert_ids == expert, axis=1)
        chosen = jnp.nonzero(member, size=slot_count, fill_value=0)[0]
        is_valid = jnp.arange(slot_count) < jnp.sum(member.astype(jnp.int32))
        picked = tokens[chosen]
        gate_sum = jnp.dot(picked.astype(jnp.float32), gate_weight[expert].astype(jnp.float32), preferred_element_type=jnp.float32)
        up_sum = jnp.dot(picked.astype(jnp.float32), up_weight[expert].astype(jnp.float32), preferred_element_type=jnp.float32)
        hidden = (jax.nn.silu(gate_sum) * up_sum).astype(jnp.bfloat16)
        hidden = jnp.where(is_valid[:, None], hidden, jnp.zeros_like(hidden))
        hidden_f = hidden.astype(jnp.float32)
        gram_sum = jnp.einsum('rf,rg->fg', hidden_f, hidden_f) / SLOTS_DEV + damping * identity
        factor = jnp.linalg.cholesky(gram_sum).T
        whitened = jnp.dot(factor, down_weight[expert].astype(jnp.float32), precision=lax.Precision.HIGHEST)
        return (factor, whitened)
    factors, whitened = lax.map(per_expert, jnp.arange(EXPERTS, dtype=jnp.int32))
    return (factors, whitened)
```

```python
import functools

import jax
import jax.numpy as jnp
from jax import lax
from jax.experimental import pallas as pl
from jax.experimental.pallas import tpu as pltpu
from jax.sharding import PartitionSpec as P

CAP = 8
CORES = 2
PANEL = 128
WINDOW = 16
damping = 0.02
highest = lax.Precision.HIGHEST
f32 = jnp.float32
bf16 = jnp.bfloat16


def reciprocal(value):
    guess = pl.reciprocal(value, approx=True)
    return guess * (2.0 - value * guess)


def factor_block(a_ref, u_ref, inverse_ref, start):
    row_in_window = lax.broadcasted_iota(jnp.int32, (WINDOW, PANEL), 0)
    lane = lax.broadcasted_iota(jnp.int32, (WINDOW, PANEL), 1)
    lane8 = lax.broadcasted_iota(jnp.int32, (8, PANEL), 1)
    row8 = lax.broadcasted_iota(jnp.int32, (8, PANEL), 0)
    groups = PANEL // 8
    per_window = WINDOW // 8
    left = [a_ref[start + 8 * i : start + 8 * i + 8, start : start + PANEL] for i in range(groups)]
    right = [(lane8 == row8 + 8 * i).astype(f32) for i in range(groups)]
    for window in range(PANEL // WINDOW):
        k = window * WINDOW
        first = window * per_window
        rows_l = jnp.concatenate(left[first : first + per_window], 0)
        rows_r = jnp.concatenate(right[first : first + per_window], 0)
        columns = [
            jnp.broadcast_to(rows_l[:, k + c : k + c + 1], (WINDOW, PANEL)) for c in range(WINDOW)
        ]
        upper_l = jnp.zeros((WINDOW, PANEL), f32)
        upper_r = jnp.zeros((WINDOW, PANEL), f32)
        pivots = jnp.zeros((WINDOW, PANEL), f32)
        for r in range(WINDOW):
            here = row_in_window == r
            pivot = columns[r][r : r + 1, :]
            ratio = jnp.where(here, 0.0, columns[r]) * reciprocal(pivot)
            pivot_l, pivot_r = rows_l[r : r + 1, :], rows_r[r : r + 1, :]
            upper_l = jnp.where(here, pivot_l, upper_l)
            upper_r = jnp.where(here, pivot_r, upper_r)
            pivots = jnp.where(here, pivot, pivots)
            rows_l = rows_l - ratio * pivot_l
            rows_r = rows_r - ratio * pivot_r
            for c in range(r + 1, WINDOW):
                columns[c] = columns[c] - ratio * columns[c][r : r + 1, :]
        inverse, root = reciprocal(pivots), lax.rsqrt(pivots)
        rows_l, rows_r = rows_l * inverse, rows_r * inverse
        u_ref[start + k : start + k + WINDOW, start : start + PANEL] = jnp.where(
            lane >= row_in_window + k, upper_l * root, 0.0
        )
        inverse_ref[k : k + WINDOW, :] = upper_r * root
        for i in range(first + per_window, groups):
            old, new_l, new_r = left[i], left[i], right[i]
            for c in range(WINDOW):
                scale = jnp.broadcast_to(old[:, k + c : k + c + 1], (8, PANEL))
                new_l = new_l - scale * rows_l[c : c + 1, :]
                new_r = new_r - scale * rows_r[c : c + 1, :]
            left[i], right[i] = new_l, new_r


def transposed_dot(a, b, precision=None):
    return lax.dot_general(
        a, b, (((0,), (0,)), ((), ())), preferred_element_type=f32, precision=precision
    )


def whiten_kernel(scale, index_ref, hidden_ref, down_ref, factor_ref, out_ref, a_ref, u_ref, inverse_ref):
    width = hidden_ref.shape[1]
    blocks = width // PANEL
    u_ref[...] = jnp.zeros_like(u_ref)
    for b in range(blocks):
        s = b * PANEL
        gram = transposed_dot(hidden_ref[:, s : s + PANEL], hidden_ref[:, s:]) * scale
        row = lax.broadcasted_iota(jnp.int32, gram.shape, 0)
        lane = lax.broadcasted_iota(jnp.int32, gram.shape, 1)
        a_ref[s : s + PANEL, s:] = jnp.where(row == lane, gram + damping, gram)
    for p in range(blocks):
        s, e = p * PANEL, (p + 1) * PANEL
        factor_block(a_ref, u_ref, inverse_ref, s)
        if e < width:
            panel = jnp.dot(
                inverse_ref[...], a_ref[s:e, e:], preferred_element_type=f32, precision=highest
            )
            u_ref[s:e, e:] = panel
            for b in range(p + 1, blocks):
                t = b * PANEL
                a_ref[t : t + PANEL, t:] = a_ref[t : t + PANEL, t:] - transposed_dot(
                    panel[:, t - e : t - e + PANEL], panel[:, t - e :], highest
                )
        rows = u_ref[s:e, s:]
        high = rows.astype(bf16)
        low = (rows - high.astype(f32)).astype(bf16)
        down = down_ref[s:, :]
        out_ref[s:e, :] = jnp.dot(high, down, preferred_element_type=f32) + jnp.dot(
            low, down, preferred_element_type=f32
        )
    share = factor_ref.shape[0]
    factor_ref[...] = u_ref[pl.ds(pl.multiple_of(index_ref[0] * share, 8), share), :]


def whiten(index, hidden, down, share, slot_total):
    width, columns = down.shape
    vmem = pl.BlockSpec(memory_space=pltpu.VMEM)
    return pl.pallas_call(
        functools.partial(whiten_kernel, 1.0 / slot_total),
        out_shape=(
            jax.ShapeDtypeStruct((share, width), f32),
            jax.ShapeDtypeStruct((width, columns), f32),
        ),
        in_specs=[pl.BlockSpec(memory_space=pltpu.SMEM), vmem, vmem],
        out_specs=(vmem, vmem),
        scratch_shapes=[
            pltpu.VMEM((width, width), f32),
            pltpu.VMEM((width, width), f32),
            pltpu.VMEM((PANEL, PANEL), f32),
        ],
        compiler_params=pltpu.CompilerParams(vmem_limit_bytes=48 * 2**20),
        name="whiten",
    )(index, hidden, down)


def hidden_kernel(index_ref, token_ref, weight_ref, out_ref):
    chunks, depth, both = weight_ref.shape
    width = both // 2
    total = None
    for j in range(chunks):
        at = pl.multiple_of(index_ref[j] * depth, depth)
        part = jnp.dot(token_ref[:, pl.ds(at, depth)], weight_ref[j], preferred_element_type=f32)
        total = part if total is None else total + part
    gate, up = total[:, :width], total[:, width:]
    hidden = (gate / (1.0 + jnp.exp(-gate)) * up).astype(bf16)
    sources = chunks // CORES
    rows = hidden.shape[0] // sources
    for k in range(sources):
        at = pl.multiple_of(index_ref[chunks + k] * rows, 16)
        out_ref[pl.ds(at, rows), :] = hidden[k * rows : (k + 1) * rows]


def project(chunk_index, tokens, weights):
    vmem = pl.BlockSpec(memory_space=pltpu.VMEM)
    return pl.pallas_call(
        hidden_kernel,
        out_shape=jax.ShapeDtypeStruct((tokens.shape[0], weights.shape[2] // 2), bf16),
        in_specs=[pl.BlockSpec(memory_space=pltpu.SMEM), vmem, vmem],
        out_specs=vmem,
        compiler_params=pltpu.CompilerParams(vmem_limit_bytes=48 * 2**20),
        name="project",
    )(chunk_index, tokens, weights)


def body(tokens, expert_ids, gate_weight, up_weight, down_weight):
    experts = lax.axis_size("expert")
    owners = experts * gate_weight.shape[0]
    dp_size = lax.axis_size("dp")
    chips = dp_size // CORES
    dp = lax.axis_index("dp")
    chip, core = dp // CORES, dp % CORES
    width = gate_weight.shape[2]
    share = width // chips

    def to_chip(x, k):
        steps = [(i, (i + k * CORES) % dp_size) for i in range(dp_size)]
        return lax.ppermute(x, "dp", steps)

    def to_core(x):
        return lax.ppermute(x, "dp", [(i, i ^ 1) for i in range(dp_size)])

    def weight_block(owner):
        at = owner * share
        return jnp.concatenate(
            [
                lax.dynamic_slice_in_dim(gate_weight[0], at, share, 1),
                lax.dynamic_slice_in_dim(up_weight[0], at, share, 1),
            ],
            1,
        )

    blocks = [weight_block(chip)]
    for k in range(1, chips):
        blocks.append(to_chip(weight_block((chip + k) % chips), k))
    sources = [(chip - k + chips) % chips for k in range(chips)]
    blocks = blocks + [to_core(block) for block in blocks]
    chunk_index = jnp.stack(
        [source * CORES + core for source in sources]
        + [source * CORES + 1 - core for source in sources]
        + sources
    ).astype(jnp.int32)

    tok_rows = tokens.shape[0]
    expert_range = jnp.arange(owners, dtype=jnp.int32)
    member = jnp.any(expert_ids[:, :, None] == expert_range[None, None, :], axis=1)
    earlier = (jnp.arange(tok_rows)[:, None] > jnp.arange(tok_rows)[None, :]).astype(jnp.int32)
    ranking = jnp.dot(earlier, member.astype(jnp.int32))
    slot_range = jnp.arange(CAP, dtype=jnp.int32)
    placing = (member[:, :, None] & (ranking[:, :, None] == slot_range[None, None, :])).astype(bf16)
    outgoing = jnp.einsum("tec,td->ecd", placing, tokens, preferred_element_type=f32).astype(bf16)
    arrived = lax.all_to_all(outgoing, "expert", split_axis=0, concat_axis=0, tiled=True)
    received = arrived.reshape(-1, arrived.shape[-1])
    slot_total = received.shape[0]

    slots = jnp.concatenate([received] + [to_chip(received, k) for k in range(1, chips)], 0)
    hidden = project(chunk_index, slots, jnp.stack(blocks))

    pieces = jnp.stack([hidden] + [to_chip(hidden, k) for k in range(1, chips)])
    ordered = jnp.roll(pieces[::-1], chip + 1, axis=0)
    whole = jnp.moveaxis(ordered, 0, 1).reshape(chips * slot_total, width)
    whole = jnp.concatenate([whole, to_core(whole)], 0)
    factor, whitened = whiten(
        dp.astype(jnp.int32)[None], whole, down_weight[0], width // dp_size, slot_total
    )
    return (factor[None], whitened[None])


def solution(mesh):
    return jax.shard_map(
        body,
        mesh=mesh,
        in_specs=(
            P(("dp", "expert"), None),
            P(("dp", "expert"), None),
            P("expert", "dp", None),
            P("expert", "dp", None),
            P("expert", None, "dp"),
        ),
        out_specs=(P("expert", "dp", None), P("expert", None, "dp")),
        check_vma=False,
    )
```

```python
import functools

import jax
import jax.numpy as jnp
from jax import lax
from jax.experimental import pallas as pl
from jax.experimental.pallas import tpu as pltpu
from jax.sharding import PartitionSpec as P

CAP = 8
CORES = 2
PANEL = 128
WINDOW = 16
damping = 0.02
highest = lax.Precision.HIGHEST
f32 = jnp.float32
bf16 = jnp.bfloat16


def reciprocal(value):
    guess = pl.reciprocal(value, approx=True)
    return guess * (2.0 - value * guess)


def factor_block(a_ref, u_ref, inverse_ref, start):
    row_in_window = lax.broadcasted_iota(jnp.int32, (WINDOW, PANEL), 0)
    lane = lax.broadcasted_iota(jnp.int32, (WINDOW, PANEL), 1)
    lane8 = lax.broadcasted_iota(jnp.int32, (8, PANEL), 1)
    row8 = lax.broadcasted_iota(jnp.int32, (8, PANEL), 0)
    groups = PANEL // 8
    per_window = WINDOW // 8
    left = [a_ref[start + 8 * i : start + 8 * i + 8, start : start + PANEL] for i in range(groups)]
    right = [(lane8 == row8 + 8 * i).astype(f32) for i in range(groups)]
    for window in range(PANEL // WINDOW):
        k = window * WINDOW
        first = window * per_window
        rows_l = jnp.concatenate(left[first : first + per_window], 0)
        rows_r = jnp.concatenate(right[first : first + per_window], 0)
        columns = [
            jnp.broadcast_to(rows_l[:, k + c : k + c + 1], (WINDOW, PANEL)) for c in range(WINDOW)
        ]
        upper_l = jnp.zeros((WINDOW, PANEL), f32)
        upper_r = jnp.zeros((WINDOW, PANEL), f32)
        pivots = jnp.zeros((WINDOW, PANEL), f32)
        for r in range(WINDOW):
            here = row_in_window == r
            pivot = columns[r][r : r + 1, :]
            ratio = jnp.where(here, 0.0, columns[r]) * reciprocal(pivot)
            pivot_l, pivot_r = rows_l[r : r + 1, :], rows_r[r : r + 1, :]
            upper_l = jnp.where(here, pivot_l, upper_l)
            upper_r = jnp.where(here, pivot_r, upper_r)
            pivots = jnp.where(here, pivot, pivots)
            rows_l = rows_l - ratio * pivot_l
            rows_r = rows_r - ratio * pivot_r
            for c in range(r + 1, WINDOW):
                columns[c] = columns[c] - ratio * columns[c][r : r + 1, :]
        inverse, root = reciprocal(pivots), lax.rsqrt(pivots)
        rows_l, rows_r = rows_l * inverse, rows_r * inverse
        u_ref[start + k : start + k + WINDOW, start : start + PANEL] = jnp.where(
            lane >= row_in_window + k, upper_l * root, 0.0
        )
        inverse_ref[k : k + WINDOW, :] = upper_r * root
        for i in range(first + per_window, groups):
            old, new_l, new_r = left[i], left[i], right[i]
            for c in range(WINDOW):
                scale = jnp.broadcast_to(old[:, k + c : k + c + 1], (8, PANEL))
                new_l = new_l - scale * rows_l[c : c + 1, :]
                new_r = new_r - scale * rows_r[c : c + 1, :]
            left[i], right[i] = new_l, new_r


def transposed_dot(a, b, precision=None):
    return lax.dot_general(
        a, b, (((0,), (0,)), ((), ())), preferred_element_type=f32, precision=precision
    )


def whiten_kernel(scale, index_ref, down_ref, *refs):
    *row_refs, factor_ref, out_ref, hidden_ref, a_ref, u_ref, inverse_ref = refs
    width = hidden_ref.shape[1]
    step = row_refs[0].shape[0]
    for i, row_ref in enumerate(row_refs):
        hidden_ref[i * step : (i + 1) * step, :] = row_ref[...]
    blocks = width // PANEL
    u_ref[...] = jnp.zeros_like(u_ref)
    for b in range(blocks):
        s = b * PANEL
        gram = transposed_dot(hidden_ref[:, s : s + PANEL], hidden_ref[:, s:]) * scale
        row = lax.broadcasted_iota(jnp.int32, gram.shape, 0)
        lane = lax.broadcasted_iota(jnp.int32, gram.shape, 1)
        a_ref[s : s + PANEL, s:] = jnp.where(row == lane, gram + damping, gram)
    for p in range(blocks):
        s, e = p * PANEL, (p + 1) * PANEL
        factor_block(a_ref, u_ref, inverse_ref, s)
        if e < width:
            panel = jnp.dot(
                inverse_ref[...], a_ref[s:e, e:], preferred_element_type=f32, precision=highest
            )
            u_ref[s:e, e:] = panel
            for b in range(p + 1, blocks):
                t = b * PANEL
                a_ref[t : t + PANEL, t:] = a_ref[t : t + PANEL, t:] - transposed_dot(
                    panel[:, t - e : t - e + PANEL], panel[:, t - e :], highest
                )
        rows = u_ref[s:e, s:]
        high = rows.astype(bf16)
        low = (rows - high.astype(f32)).astype(bf16)
        down = down_ref[s:, :]
        out_ref[s:e, :] = jnp.dot(high, down, preferred_element_type=f32) + jnp.dot(
            low, down, preferred_element_type=f32
        )
    share = factor_ref.shape[0]
    factor_ref[...] = u_ref[pl.ds(pl.multiple_of(index_ref[0] * share, 8), share), :]


def whiten(index, rows, down, share, slot_total):
    width, columns = down.shape
    vmem = pl.BlockSpec(memory_space=pltpu.VMEM)
    return pl.pallas_call(
        functools.partial(whiten_kernel, 1.0 / slot_total),
        out_shape=(
            jax.ShapeDtypeStruct((share, width), f32),
            jax.ShapeDtypeStruct((width, columns), f32),
        ),
        in_specs=[pl.BlockSpec(memory_space=pltpu.SMEM), vmem] + [vmem] * len(rows),
        out_specs=(vmem, vmem),
        scratch_shapes=[
            pltpu.VMEM((len(rows) * rows[0].shape[0], width), bf16),
            pltpu.VMEM((width, width), f32),
            pltpu.VMEM((width, width), f32),
            pltpu.VMEM((PANEL, PANEL), f32),
        ],
        compiler_params=pltpu.CompilerParams(vmem_limit_bytes=48 * 2**20),
        name="whiten",
    )(index, down, *rows)


def project_kernel(index_ref, token_ref, *refs):
    *weight_refs, out_ref = refs
    chips, slots, both = out_ref.shape
    width = both // 2
    depth = weight_refs[0].shape[0]
    chip, core = index_ref[0], index_ref[1]
    starts = [core * depth, (1 - core) * depth]
    for k in range(chips):
        owner = lax.rem(chip + k + 1, chips)
        rows = pl.ds(pl.multiple_of(owner * slots, 16), slots)
        for half in range(2):
            total = None
            for j in range(CORES):
                part = jnp.dot(
                    token_ref[rows, pl.ds(pl.multiple_of(starts[j], depth), depth)],
                    weight_refs[2 * j + half][...],
                    preferred_element_type=f32,
                )
                total = part if total is None else total + part
            out_ref[k, :, half * width : (half + 1) * width] = total


def project(index, tokens, weights, chips):
    vmem = pl.BlockSpec(memory_space=pltpu.VMEM)
    both = 2 * weights[0].shape[1]
    return pl.pallas_call(
        project_kernel,
        out_shape=jax.ShapeDtypeStruct((chips, tokens.shape[0] // chips, both), f32),
        in_specs=[pl.BlockSpec(memory_space=pltpu.SMEM)] + [vmem] * (1 + len(weights)),
        out_specs=vmem,
        compiler_params=pltpu.CompilerParams(vmem_limit_bytes=48 * 2**20),
        name="project",
    )(index, tokens, *weights)


def body(tokens, expert_ids, gate_weight, up_weight, down_weight):
    experts = lax.axis_size("expert")
    owners = experts * gate_weight.shape[0]
    dp_size = lax.axis_size("dp")
    chips = dp_size // CORES
    dp = lax.axis_index("dp")
    chip, core = dp // CORES, dp % CORES
    width = gate_weight.shape[2]
    tok_rows, model = tokens.shape

    def to_chip(x, k):
        steps = [(i, (i + k * CORES) % dp_size) for i in range(dp_size)]
        return lax.ppermute(x, "dp", steps)

    def to_core(x):
        return lax.ppermute(x, "dp", [(i, i ^ 1) for i in range(dp_size)])

    gate, up = gate_weight[0], up_weight[0]
    weights = [gate, up, to_core(gate), to_core(up)]

    expert_range = jnp.arange(owners, dtype=jnp.int32)
    member = jnp.any(expert_ids[:, :, None] == expert_range[None, None, :], axis=1)
    earlier = (jnp.arange(tok_rows)[:, None] > jnp.arange(tok_rows)[None, :]).astype(jnp.int32)
    ranking = jnp.dot(earlier, member.astype(jnp.int32))
    slot_range = jnp.arange(CAP, dtype=jnp.int32)
    placing = (member[:, :, None] & (ranking[:, :, None] == slot_range[None, None, :])).astype(bf16)
    outgoing = jnp.einsum(
        "tec,tyd->yecd",
        placing,
        tokens.reshape(tok_rows, chips, model // chips),
        preferred_element_type=f32,
    ).astype(bf16)
    groups = [
        [(y * CORES + c) * experts + e for y in range(chips) for e in range(experts)]
        for c in range(CORES)
    ]
    arrived = lax.all_to_all(
        outgoing.reshape(chips * owners, CAP, model // chips),
        ("dp", "expert"),
        split_axis=0,
        concat_axis=0,
        axis_index_groups=groups,
        tiled=True,
    )
    received = arrived.reshape(-1, model // chips)
    slot_total = received.shape[0] // chips

    index = jnp.stack([chip, core]).astype(jnp.int32)
    partial = project(index, received, weights, chips)
    total = partial[chips - 1]
    for k in range(1, chips):
        total = total + to_chip(partial[k - 1], k)
    gate_sum, up_sum = total[:, :width], total[:, width:]
    hidden = (gate_sum / (1.0 + jnp.exp(-gate_sum)) * up_sum).astype(bf16)
    rows = [hidden] + [to_chip(hidden, k) for k in range(1, chips)]
    rows = rows + [to_core(row) for row in rows]
    factor, whitened = whiten(
        dp.astype(jnp.int32)[None], rows, down_weight[0], width // dp_size, slot_total
    )
    return (factor[None], whitened[None])


def solution(mesh):
    return jax.shard_map(
        body,
        mesh=mesh,
        in_specs=(
            P(("dp", "expert"), None),
            P(("dp", "expert"), None),
            P("expert", "dp", None),
            P("expert", "dp", None),
            P("expert", None, "dp"),
        ),
        out_specs=(P("expert", "dp", None), P("expert", None, "dp")),
        check_vma=False,
    )
```

```python
import functools

import jax
import jax.numpy as jnp
from jax import lax
from jax.experimental import pallas as pl
from jax.experimental.pallas import tpu as pltpu
from jax.sharding import PartitionSpec as P

CAP = 8
CORES = 2
PANEL = 128
WINDOW = 16
SUPER = 64
CHUNK = 256
damping = 0.02
highest = lax.Precision.HIGHEST
f32 = jnp.float32
bf16 = jnp.bfloat16


def reciprocal(value):
    return pl.reciprocal(value, approx=True)


def transposed_dot(a, b, precision=None):
    return lax.dot_general(a, b, (((0,), (0,)), ((), ())), preferred_element_type=f32, precision=precision)

def tree(terms):
    while len(terms) > 1:
        terms = [terms[i] + terms[i + 1] if i + 1 < len(terms) else terms[i] for i in range(0, len(terms), 2)]
    return terms[0]

def eliminate(columns, sides):
    row8 = lax.broadcasted_iota(jnp.int32, (8, PANEL), 0)
    groups = WINDOW // 8
    uppers = [[jnp.zeros((8, PANEL), f32) for _ in range(groups)] for _ in sides]
    sides = [list(side) for side in sides]
    scales = []
    for r in range(0, WINDOW, 2):
        h, t = r // 8, r % 8
        first, second = columns[r], columns[r + 1]
        a, b, c = first[h][t : t + 1], first[h][t + 1 : t + 2], second[h][t + 1 : t + 2]
        det = a * c - b * b
        q = reciprocal(det)
        root_a = lax.rsqrt(a)
        inv_a = root_a * root_a
        root_d = lax.rsqrt(det * inv_a)
        slope = b * inv_a
        scales.append((a * q, b * q, c * q))
        l0, l1 = [], []
        pair = (row8 == t) | (row8 == t + 1)
        for g in range(groups):
            f, d = first[g], second[g]
            if g == h:
                f, d = jnp.where(pair, 0.0, f), jnp.where(pair, 0.0, d)
            l0.append((c * f - b * d) * q)
            l1.append((a * d - b * f) * q)
        for j in range(r + 2, WINDOW):
            x, y = columns[j][h][t : t + 1], columns[j][h][t + 1 : t + 2]
            columns[j] = [columns[j][g] - (l0[g] * x + l1[g] * y) for g in range(groups)]
        for n, side in enumerate(sides):
            x, y = side[h][t : t + 1], side[h][t + 1 : t + 2]
            uppers[n][h] = jnp.where(row8 == t, x * root_a, jnp.where(row8 == t + 1, (y - slope * x) * root_d, uppers[n][h]))
            sides[n] = [side[g] - (l0[g] * x + l1[g] * y) for g in range(groups)]
    solved = []
    for side in sides:
        rows = []
        for r in range(0, WINDOW, 2):
            h, t = r // 8, r % 8
            aq, bq, cq = scales[r // 2]
            x, y = side[h][t : t + 1], side[h][t + 1 : t + 2]
            rows += [cq * x - bq * y, aq * y - bq * x]
        solved.append(rows)
    return uppers, solved

def factor_steps(block, result, zero):
    lane8 = lax.broadcasted_iota(jnp.int32, (8, PANEL), 1)
    row8 = lax.broadcasted_iota(jnp.int32, (8, PANEL), 0)
    groups = PANEL // 8
    per_window = WINDOW // 8
    left = [block[8 * i : 8 * i + 8] for i in range(groups)]
    right = [(lane8 == row8 + 8 * i).astype(f32) for i in range(groups)]
    uppers, inverses = [], []
    for window in range(PANEL // WINDOW):
        k = window * WINDOW
        first = window * per_window
        mine = range(first, first + per_window)
        columns = [[jnp.broadcast_to(left[g][:, k + c : k + c + 1], (8, PANEL)) + zero for g in mine] for c in range(WINDOW)]
        (up_l, up_r), (w_l, w_r) = eliminate(columns, [[left[g] for g in mine], [right[g] for g in mine]])
        uppers += [jnp.where(lane8 >= row8 + 8 * g, u, 0.0) for g, u in zip(mine, up_l)]
        inverses += up_r
        near = min(groups, (k // SUPER + 1) * SUPER // 8)
        for i in range(first + per_window, near):
            scale = [jnp.broadcast_to(left[i][:, k + c : k + c + 1], (8, PANEL)) for c in range(WINDOW)]
            left[i] = left[i] - tree([scale[c] * w_l[c] for c in range(WINDOW)])
            right[i] = right[i] - tree([scale[c] * w_r[c] for c in range(WINDOW)])
        if (k + WINDOW) % SUPER == 0 and near < groups:
            parts = SUPER // 8
            up = jnp.concatenate(uppers[-parts:], 0)
            inv = jnp.concatenate(inverses[-parts:], 0)
            mult = up[:, near * 8 :]
            chg_l = transposed_dot(mult, up, highest)
            chg_r = transposed_dot(mult, inv, highest)
            for i in range(near, groups):
                o = (i - near) * 8
                left[i] = left[i] - chg_l[o : o + 8]
                right[i] = right[i] - chg_r[o : o + 8]
        if window == PANEL // WINDOW - 1:
            result.append(jnp.concatenate(uppers, 0))
            result.append(jnp.concatenate(inverses, 0))
        yield

def whiten_kernel(scale, index_ref, down_ref, *refs):
    *row_refs, factor_ref, out_ref, hidden_ref, a_ref, u_ref, inverse_ref = refs
    width = hidden_ref.shape[1]
    step = row_refs[0].shape[0]
    for i, row_ref in enumerate(row_refs):
        hidden_ref[i * step : (i + 1) * step, :] = row_ref[...]
    blocks = width // PANEL
    steps = PANEL // WINDOW
    zero = jnp.full((8, PANEL), jnp.where(index_ref[0] < 0, 1.0, 0.0), f32)

    def gram(b, lo, hi):
        s = b * PANEL
        g = transposed_dot(hidden_ref[:, s : s + PANEL], hidden_ref[:, lo:hi]) * scale
        row = lax.broadcasted_iota(jnp.int32, g.shape, 0) + s
        lane = lax.broadcasted_iota(jnp.int32, g.shape, 1) + lo
        return jnp.where(row == lane, g + damping, g)

    def chunks(start):
        return [(c, min(c + CHUNK, width)) for c in range(start, width, CHUNK)]

    def store_gram(b, lo, hi):
        a_ref[b * PANEL : (b + 1) * PANEL, lo:hi] = gram(b, lo, hi)

    def panel(p, lo, hi):
        s, e = p * PANEL, (p + 1) * PANEL
        u_ref[s:e, lo:hi] = jnp.dot(inverse_ref[p % 2], a_ref[s:e, lo:hi], preferred_element_type=f32, precision=highest)

    def trail(p, b, lo, hi):
        s, e, t = p * PANEL, (p + 1) * PANEL, b * PANEL
        a_ref[t : t + PANEL, lo:hi] = a_ref[t : t + PANEL, lo:hi] - transposed_dot(u_ref[s:e, t : t + PANEL], u_ref[s:e, lo:hi], highest)

    def output(p):
        s, e = p * PANEL, (p + 1) * PANEL
        rows = u_ref[s:e, s:]
        high = rows.astype(bf16)
        low = (rows - high.astype(f32)).astype(bf16)
        down = down_ref[s:, :]
        out_ref[s:e, :] = jnp.dot(high, down, preferred_element_type=f32) + jnp.dot(low, down, preferred_element_type=f32)

    def clear(p):
        if p: u_ref[p * PANEL : (p + 1) * PANEL, : p * PANEL] = jnp.zeros((PANEL, p * PANEL), f32)

    block = gram(0, 0, PANEL)
    work = [functools.partial(store_gram, 0, lo, hi) for lo, hi in chunks(PANEL)]
    for b in range(1, blocks):
        work += [functools.partial(store_gram, b, lo, hi) for lo, hi in chunks(b * PANEL)]
        work.append(functools.partial(clear, b))
    for p in range(blocks):
        s, e = p * PANEL, (p + 1) * PANEL
        result = []
        done = 0
        for i, _ in enumerate(factor_steps(block, result, zero)):
            upto = len(work) * (i + 1) // steps
            for job in work[done:upto]: job()
            done = upto
        u_ref[s:e, s:e] = result[0]
        if e < width:
            inverse_ref[p % 2] = result[1]
            nxt = jnp.dot(result[1], a_ref[s:e, e:e+PANEL], preferred_element_type=f32, precision=highest)
            u_ref[s:e, e:e+PANEL] = nxt
            block = a_ref[e:e+PANEL, e:e+PANEL] - transposed_dot(nxt, nxt, highest)
            f = e + PANEL
            work = [functools.partial(panel, p, lo, hi) for lo, hi in chunks(f)]
            work += [functools.partial(trail, p, p + 1, lo, hi) for lo, hi in chunks(f)]
            for b in range(p + 2, blocks):
                work += [functools.partial(trail, p, b, lo, hi) for lo, hi in chunks(b * PANEL)]
            work.append(functools.partial(output, p))
        else:
            output(p)
    share = factor_ref.shape[0]
    factor_ref[...] = u_ref[pl.ds(pl.multiple_of(index_ref[0] * share, 8), share), :]

def whiten(index, rows, down, share, slot_total):
    width, columns = down.shape
    vmem = pl.BlockSpec(memory_space=pltpu.VMEM)
    return pl.pallas_call(
        functools.partial(whiten_kernel, 1.0 / slot_total),
        out_shape=(jax.ShapeDtypeStruct((share, width), f32), jax.ShapeDtypeStruct((width, columns), f32)),
        in_specs=[pl.BlockSpec(memory_space=pltpu.SMEM), vmem] + [vmem] * len(rows),
        out_specs=(vmem, vmem),
        scratch_shapes=[
            pltpu.VMEM((len(rows) * rows[0].shape[0], width), bf16),
            pltpu.VMEM((width, width), f32),
            pltpu.VMEM((width, width), f32),
            pltpu.VMEM((2, PANEL, PANEL), f32),
        ],
        compiler_params=pltpu.CompilerParams(vmem_limit_bytes=48 * 2**20),
        name="whiten",
    )(index, down, *rows)


def project_kernel(index_ref, token_ref, *refs):
    *weight_refs, out_ref = refs
    chips, slots, both = out_ref.shape
    width = both // 2
    depth = weight_refs[0].shape[0]
    chip, core = index_ref[0], index_ref[1]
    starts = [core * depth, (1 - core) * depth]
    for k in range(chips):
        owner = lax.rem(chip + k + 1, chips)
        rows = pl.ds(pl.multiple_of(owner * slots, 16), slots)
        for half in range(2):
            total = None
            for j in range(CORES):
                part = jnp.dot(
                    token_ref[rows, pl.ds(pl.multiple_of(starts[j], depth), depth)],
                    weight_refs[2 * j + half][...],
                    preferred_element_type=f32,
                )
                total = part if total is None else total + part
            out_ref[k, :, half * width : (half + 1) * width] = total


def project(index, tokens, weights, chips):
    vmem = pl.BlockSpec(memory_space=pltpu.VMEM)
    both = 2 * weights[0].shape[1]
    return pl.pallas_call(
        project_kernel,
        out_shape=jax.ShapeDtypeStruct((chips, tokens.shape[0] // chips, both), f32),
        in_specs=[pl.BlockSpec(memory_space=pltpu.SMEM)] + [vmem] * (1 + len(weights)),
        out_specs=vmem,
        compiler_params=pltpu.CompilerParams(vmem_limit_bytes=48 * 2**20),
        name="project",
    )(index, tokens, *weights)


def body(tokens, expert_ids, gate_weight, up_weight, down_weight):
    experts = lax.axis_size("expert")
    owners = experts * gate_weight.shape[0]
    dp_size = lax.axis_size("dp")
    chips = dp_size // CORES
    dp = lax.axis_index("dp")
    chip, core = dp // CORES, dp % CORES
    width = gate_weight.shape[2]
    tok_rows, model = tokens.shape

    def to_chip(x, k):
        steps = [(i, (i + k * CORES) % dp_size) for i in range(dp_size)]
        return lax.ppermute(x, "dp", steps)

    def to_core(x):
        return lax.ppermute(x, "dp", [(i, i ^ 1) for i in range(dp_size)])

    gate, up = gate_weight[0], up_weight[0]
    weights = [gate, up, to_core(gate), to_core(up)]

    expert_range = jnp.arange(owners, dtype=jnp.int32)
    member = jnp.any(expert_ids[:, :, None] == expert_range[None, None, :], axis=1)
    earlier = (jnp.arange(tok_rows)[:, None] > jnp.arange(tok_rows)[None, :]).astype(jnp.int32)
    ranking = jnp.dot(earlier, member.astype(jnp.int32))
    slot_range = jnp.arange(CAP, dtype=jnp.int32)
    placing = (member[:, :, None] & (ranking[:, :, None] == slot_range[None, None, :])).astype(bf16)
    outgoing = jnp.einsum(
        "tec,tyd->yecd",
        placing,
        tokens.reshape(tok_rows, chips, model // chips),
        preferred_element_type=f32,
    ).astype(bf16)
    groups = [
        [(y * CORES + c) * experts + e for y in range(chips) for e in range(experts)]
        for c in range(CORES)
    ]
    arrived = lax.all_to_all(
        outgoing.reshape(chips * owners, CAP, model // chips),
        ("dp", "expert"),
        split_axis=0,
        concat_axis=0,
        axis_index_groups=groups,
        tiled=True,
    )
    received = arrived.reshape(-1, model // chips)
    slot_total = received.shape[0] // chips

    index = jnp.stack([chip, core]).astype(jnp.int32)
    partial = project(index, received, weights, chips)
    total = partial[chips - 1]
    for k in range(1, chips):
        total = total + to_chip(partial[k - 1], k)
    gate_sum, up_sum = total[:, :width], total[:, width:]
    hidden = (gate_sum / (1.0 + jnp.exp(-gate_sum)) * up_sum).astype(bf16)
    rows = [hidden] + [to_chip(hidden, k) for k in range(1, chips)]
    rows = rows + [to_core(row) for row in rows]
    factor, whitened = whiten(
        dp.astype(jnp.int32)[None], rows, down_weight[0], width // dp_size, slot_total
    )
    return (factor[None], whitened[None])


def solution(mesh):
    return jax.shard_map(
        body,
        mesh=mesh,
        in_specs=(
            P(("dp", "expert"), None),
            P(("dp", "expert"), None),
            P("expert", "dp", None),
            P("expert", "dp", None),
            P("expert", None, "dp"),
        ),
        out_specs=(P("expert", "dp", None), P("expert", None, "dp")),
        check_vma=False,
    )
```

```python
import functools

import jax
import jax.numpy as jnp
from jax import lax
from jax.experimental import pallas as pl
from jax.experimental.pallas import tpu as pltpu
from jax.sharding import PartitionSpec as P

CAP = 8
CORES = 2
PANEL = 128
WINDOW = 16
SUPER = 64
CHUNK = 256
damping = 0.02
highest = lax.Precision.HIGHEST
f32 = jnp.float32
bf16 = jnp.bfloat16
f16 = jnp.float16
LINK_SCALE = 32.0


def reciprocal(value):
    return pl.reciprocal(value, approx=True)


def transposed_dot(a, b, precision=None):
    return lax.dot_general(a, b, (((0,), (0,)), ((), ())), preferred_element_type=f32, precision=precision)

def tree(terms):
    while len(terms) > 1:
        terms = [terms[i] + terms[i + 1] if i + 1 < len(terms) else terms[i] for i in range(0, len(terms), 2)]
    return terms[0]

def eliminate(columns, sides):
    row8 = lax.broadcasted_iota(jnp.int32, (8, PANEL), 0)
    groups = WINDOW // 8
    uppers = [[jnp.zeros((8, PANEL), f32) for _ in range(groups)] for _ in sides]
    sides = [list(side) for side in sides]
    scales = []
    for r in range(0, WINDOW, 2):
        h, t = r // 8, r % 8
        first, second = columns[r], columns[r + 1]
        a, b, c = first[h][t : t + 1], first[h][t + 1 : t + 2], second[h][t + 1 : t + 2]
        det = a * c - b * b
        q = reciprocal(det)
        root_a = lax.rsqrt(a)
        inv_a = root_a * root_a
        root_d = lax.rsqrt(det * inv_a)
        slope = b * inv_a
        scales.append((a * q, b * q, c * q))
        l0, l1 = [], []
        pair = (row8 == t) | (row8 == t + 1)
        for g in range(groups):
            f, d = first[g], second[g]
            if g == h:
                f, d = jnp.where(pair, 0.0, f), jnp.where(pair, 0.0, d)
            l0.append((c * f - b * d) * q)
            l1.append((a * d - b * f) * q)
        for j in range(r + 2, WINDOW):
            x, y = columns[j][h][t : t + 1], columns[j][h][t + 1 : t + 2]
            columns[j] = [columns[j][g] - (l0[g] * x + l1[g] * y) for g in range(groups)]
        for n, side in enumerate(sides):
            x, y = side[h][t : t + 1], side[h][t + 1 : t + 2]
            uppers[n][h] = jnp.where(row8 == t, x * root_a, jnp.where(row8 == t + 1, (y - slope * x) * root_d, uppers[n][h]))
            sides[n] = [side[g] - (l0[g] * x + l1[g] * y) for g in range(groups)]
    solved = []
    for side in sides:
        rows = []
        for r in range(0, WINDOW, 2):
            h, t = r // 8, r % 8
            aq, bq, cq = scales[r // 2]
            x, y = side[h][t : t + 1], side[h][t + 1 : t + 2]
            rows += [cq * x - bq * y, aq * y - bq * x]
        solved.append(rows)
    return uppers, solved

def factor_steps(block, result, zero):
    lane8 = lax.broadcasted_iota(jnp.int32, (8, PANEL), 1)
    row8 = lax.broadcasted_iota(jnp.int32, (8, PANEL), 0)
    groups = PANEL // 8
    per_window = WINDOW // 8
    left = [block[8 * i : 8 * i + 8] for i in range(groups)]
    right = [(lane8 == row8 + 8 * i).astype(f32) for i in range(groups)]
    uppers, inverses = [], []
    for window in range(PANEL // WINDOW):
        k = window * WINDOW
        first = window * per_window
        mine = range(first, first + per_window)
        columns = [[jnp.broadcast_to(left[g][:, k + c : k + c + 1], (8, PANEL)) + zero if g == first else jnp.broadcast_to(left[g][:, k + c : k + c + 1], (8, PANEL)) for g in mine] for c in range(WINDOW)]
        (up_l, up_r), (w_l, w_r) = eliminate(columns, [[left[g] for g in mine], [right[g] for g in mine]])
        uppers += [jnp.where(lane8 >= row8 + 8 * g, u, 0.0) for g, u in zip(mine, up_l)]
        inverses += up_r
        near = min(groups, (k // SUPER + 1) * SUPER // 8)
        for i in range(first + per_window, near):
            scale = [jnp.broadcast_to(left[i][:, k + c : k + c + 1], (8, PANEL)) for c in range(WINDOW)]
            left[i] = left[i] - tree([scale[c] * w_l[c] for c in range(WINDOW)])
            right[i] = right[i] - tree([scale[c] * w_r[c] for c in range(WINDOW)])
        if (k + WINDOW) % SUPER == 0 and near < groups:
            parts = SUPER // 8
            up = jnp.concatenate(uppers[-parts:], 0)
            inv = jnp.concatenate(inverses[-parts:], 0)
            mult = up[:, near * 8 :]
            chg_l = transposed_dot(mult, up, highest)
            chg_r = transposed_dot(mult, inv, highest)
            for i in range(near, groups):
                o = (i - near) * 8
                left[i] = left[i] - chg_l[o : o + 8]
                right[i] = right[i] - chg_r[o : o + 8]
        if (k + WINDOW) % SUPER == 0:
            result.append((jnp.concatenate(uppers[-SUPER // 8 :], 0), jnp.concatenate(inverses[-SUPER // 8 :], 0)))
        yield

def whiten_kernel(scale, index_ref, down_ref, *refs):
    *row_refs, factor_ref, out_ref, hidden_ref, a_ref, u_ref, inverse_ref = refs
    width = hidden_ref.shape[1]
    step = row_refs[0].shape[0]
    for i, row_ref in enumerate(row_refs):
        hidden_ref[i * step : (i + 1) * step, :] = row_ref[...]
    blocks = width // PANEL
    steps = PANEL // WINDOW
    zero = jnp.full((8, PANEL), jnp.where(index_ref[0] < 0, 1.0, 0.0), f32)

    def gram(b, lo, hi):
        s = b * PANEL
        g = transposed_dot(hidden_ref[:, s : s + PANEL], hidden_ref[:, lo:hi]) * scale
        row = lax.broadcasted_iota(jnp.int32, g.shape, 0) + s
        lane = lax.broadcasted_iota(jnp.int32, g.shape, 1) + lo
        return jnp.where(row == lane, g + damping, g)

    def chunks(start):
        return [(c, min(c + CHUNK, width)) for c in range(start, width, CHUNK)]

    def store_gram(b, lo, hi):
        a_ref[b * PANEL : (b + 1) * PANEL, lo:hi] = gram(b, lo, hi)

    def panel(p, lo, hi):
        s, e = p * PANEL, (p + 1) * PANEL
        u_ref[s:e, lo:hi] = jnp.dot(inverse_ref[p % 2], a_ref[s:e, lo:hi], preferred_element_type=f32, precision=highest)

    def trail(p, b, lo, hi):
        s, e, t = p * PANEL, (p + 1) * PANEL, b * PANEL
        a_ref[t : t + PANEL, lo:hi] = a_ref[t : t + PANEL, lo:hi] - transposed_dot(u_ref[s:e, t : t + PANEL], u_ref[s:e, lo:hi], highest)

    def output(p):
        s, e = p * PANEL, (p + 1) * PANEL
        rows = u_ref[s:e, s:]
        high = rows.astype(bf16)
        low = (rows - high.astype(f32)).astype(bf16)
        down = down_ref[s:, :]
        out_ref[s:e, :] = jnp.dot(high, down, preferred_element_type=f32) + jnp.dot(low, down, preferred_element_type=f32)

    def clear(p):
        if p: u_ref[p * PANEL : (p + 1) * PANEL, : p * PANEL] = jnp.zeros((PANEL, p * PANEL), f32)

    block = gram(0, 0, PANEL)
    work = [functools.partial(store_gram, 0, lo, hi) for lo, hi in chunks(PANEL)]
    for b in range(1, blocks):
        work += [functools.partial(store_gram, b, lo, hi) for lo, hi in chunks(b * PANEL)]
        work.append(functools.partial(clear, b))
    def first_half(p, upper, inverse):
        s, e = p * PANEL, (p + 1) * PANEL
        m = s + SUPER
        u_ref[s:m, s:e] = upper
        if e < width:
            inverse_ref[p % 2, :SUPER] = inverse
            a_next = a_ref[s:m, e : e + PANEL]
            u_ref[s:m, e : e + PANEL] = jnp.dot(inverse[:, :SUPER], a_next, preferred_element_type=f32, precision=highest)

    def first_gram(p):
        s, e = p * PANEL, (p + 1) * PANEL
        top = u_ref[s : s + SUPER, e : e + PANEL]
        a_ref[e : e + PANEL, e : e + PANEL] = a_ref[e : e + PANEL, e : e + PANEL] - transposed_dot(top, top, highest)

    half = SUPER // WINDOW
    for p in range(blocks):
        s, e = p * PANEL, (p + 1) * PANEL
        m = s + SUPER
        result = []
        done = 0
        for i, _ in enumerate(factor_steps(block, result, zero)):
            if i == half:
                first_half(p, *result[0])
            if i == half + 1 and e < width:
                first_gram(p)
            upto = len(work) * (i + 1) // steps
            for job in work[done:upto]: job()
            done = upto
        upper, inverse = result[1]
        u_ref[m:e, s:e] = upper
        if e < width:
            inverse_ref[p % 2, SUPER:] = inverse
            low = jnp.dot(inverse, a_ref[s:e, e:e+PANEL], preferred_element_type=f32, precision=highest)
            u_ref[m:e, e:e+PANEL] = low
            block = jnp.concatenate([
                a_ref[e + o : e + o + SUPER, e : e + PANEL] - transposed_dot(low[:, o : o + SUPER], low, highest)
                for o in range(0, PANEL, SUPER)], 0)
            f = e + PANEL
            work = [functools.partial(panel, p, lo, hi) for lo, hi in chunks(f)]
            work += [functools.partial(trail, p, p + 1, lo, hi) for lo, hi in chunks(f)]
            for b in range(p + 2, blocks):
                work += [functools.partial(trail, p, b, lo, hi) for lo, hi in chunks(b * PANEL)]
            work.append(functools.partial(output, p))
        else:
            output(p)
    share = factor_ref.shape[0]
    factor_ref[...] = u_ref[pl.ds(pl.multiple_of(index_ref[0] * share, 8), share), :]

def whiten(index, rows, down, share, slot_total):
    width, columns = down.shape
    vmem = pl.BlockSpec(memory_space=pltpu.VMEM)
    return pl.pallas_call(
        functools.partial(whiten_kernel, 1.0 / slot_total),
        out_shape=(jax.ShapeDtypeStruct((share, width), f32), jax.ShapeDtypeStruct((width, columns), f32)),
        in_specs=[pl.BlockSpec(memory_space=pltpu.SMEM), vmem] + [vmem] * len(rows),
        out_specs=(vmem, vmem),
        scratch_shapes=[
            pltpu.VMEM((len(rows) * rows[0].shape[0], width), bf16),
            pltpu.VMEM((width, width), f32),
            pltpu.VMEM((width, width), f32),
            pltpu.VMEM((2, PANEL, PANEL), f32),
        ],
        compiler_params=pltpu.CompilerParams(vmem_limit_bytes=48 * 2**20),
        name="whiten",
    )(index, down, *rows)


def project_kernel(index_ref, token_ref, *refs):
    *weight_refs, send_ref, keep_ref = refs
    slots, both = keep_ref.shape
    chips = send_ref.shape[0] + 1
    width = both // 2
    depth = weight_refs[0].shape[0]
    chip, core = index_ref[0], index_ref[1]
    starts = [core * depth, (1 - core) * depth]
    for k in range(chips):
        owner = lax.rem(chip + k + 1, chips)
        rows = pl.ds(pl.multiple_of(owner * slots, 16), slots)
        for half in range(2):
            total = None
            for j in range(CORES):
                part = jnp.dot(
                    token_ref[rows, pl.ds(pl.multiple_of(starts[j], depth), depth)],
                    weight_refs[2 * j + half][...],
                    preferred_element_type=f32,
                )
                total = part if total is None else total + part
            columns = slice(half * width, (half + 1) * width)
            if k < chips - 1:
                send_ref[k, :, columns] = total * LINK_SCALE
            else:
                keep_ref[:, columns] = total


def project(index, tokens, weights, chips):
    vmem = pl.BlockSpec(memory_space=pltpu.VMEM)
    both = 2 * weights[0].shape[1]
    slots = tokens.shape[0] // chips
    return pl.pallas_call(
        project_kernel,
        out_shape=(
            jax.ShapeDtypeStruct((chips - 1, slots, both), f32),
            jax.ShapeDtypeStruct((slots, both), f32),
        ),
        in_specs=[pl.BlockSpec(memory_space=pltpu.SMEM)] + [vmem] * (1 + len(weights)),
        out_specs=(vmem, vmem),
        compiler_params=pltpu.CompilerParams(vmem_limit_bytes=48 * 2**20),
        name="project",
    )(index, tokens, *weights)


def body(tokens, expert_ids, gate_weight, up_weight, down_weight):
    experts = lax.axis_size("expert")
    owners = experts * gate_weight.shape[0]
    dp_size = lax.axis_size("dp")
    chips = dp_size // CORES
    dp = lax.axis_index("dp")
    chip, core = dp // CORES, dp % CORES
    width = gate_weight.shape[2]
    tok_rows, model = tokens.shape

    def to_chip(x, k):
        steps = [(i, (i + k * CORES) % dp_size) for i in range(dp_size)]
        return lax.ppermute(x, "dp", steps)

    def to_core(x):
        return lax.ppermute(x, "dp", [(i, i ^ 1) for i in range(dp_size)])

    gate, up = gate_weight[0], up_weight[0]
    weights = [gate, up, to_core(gate), to_core(up)]

    expert_range = jnp.arange(owners, dtype=jnp.int32)
    member = jnp.any(expert_ids[:, :, None] == expert_range[None, None, :], axis=1)
    earlier = (jnp.arange(tok_rows)[:, None] > jnp.arange(tok_rows)[None, :]).astype(jnp.int32)
    ranking = jnp.dot(earlier, member.astype(jnp.int32))
    slot_range = jnp.arange(CAP, dtype=jnp.int32)
    placing = (member[:, :, None] & (ranking[:, :, None] == slot_range[None, None, :])).astype(bf16)
    outgoing = jnp.einsum(
        "tec,tyd->yecd",
        placing,
        tokens.reshape(tok_rows, chips, model // chips),
        preferred_element_type=f32,
    ).astype(bf16)
    groups = [
        [(y * CORES + c) * experts + e for y in range(chips) for e in range(experts)]
        for c in range(CORES)
    ]
    arrived = lax.all_to_all(
        outgoing.reshape(chips * owners, CAP, model // chips),
        ("dp", "expert"),
        split_axis=0,
        concat_axis=0,
        axis_index_groups=groups,
        tiled=True,
    )
    received = arrived.reshape(-1, model // chips)
    slot_total = received.shape[0] // chips

    index = jnp.stack([chip, core]).astype(jnp.int32)
    sent, total = project(index, received, weights, chips)
    for k in range(1, chips):
        total = total + to_chip(sent[k - 1].astype(f16), k).astype(f32) * (1.0 / LINK_SCALE)
    gate_sum, up_sum = total[:, :width], total[:, width:]
    hidden = (gate_sum / (1.0 + jnp.exp(-gate_sum)) * up_sum).astype(bf16)
    rows = [hidden] + [to_chip(hidden, k) for k in range(1, chips)]
    rows = rows + [to_core(row) for row in rows]
    factor, whitened = whiten(
        dp.astype(jnp.int32)[None], rows, down_weight[0], width // dp_size, slot_total
    )
    return (factor[None], whitened[None])


def solution(mesh):
    return jax.shard_map(
        body,
        mesh=mesh,
        in_specs=(
            P(("dp", "expert"), None),
            P(("dp", "expert"), None),
            P("expert", "dp", None),
            P("expert", "dp", None),
            P("expert", None, "dp"),
        ),
        out_specs=(P("expert", "dp", None), P("expert", None, "dp")),
        check_vma=False,
    )
```

```python
import functools

import jax
import jax.numpy as jnp
from jax import lax
from jax.experimental import pallas as pl
from jax.experimental.pallas import tpu as pltpu
from jax.sharding import PartitionSpec as P

CAP = 8
CORES = 2
PANEL = 128
WINDOW = 16
SUPER = 64
CHUNK = 256
damping = 0.02
highest = lax.Precision.HIGHEST
f32 = jnp.float32
bf16 = jnp.bfloat16
f16 = jnp.float16
LINK_SCALE = 32.0


def reciprocal(value):
    return pl.reciprocal(value, approx=True)


def transposed_dot(a, b, precision=None):
    return lax.dot_general(a, b, (((0,), (0,)), ((), ())), preferred_element_type=f32, precision=precision)

def tree(terms):
    while len(terms) > 1:
        terms = [terms[i] + terms[i + 1] if i + 1 < len(terms) else terms[i] for i in range(0, len(terms), 2)]
    return terms[0]

def eliminate(columns, sides):
    row8 = lax.broadcasted_iota(jnp.int32, (8, PANEL), 0)
    groups = WINDOW // 8
    uppers = [[jnp.zeros((8, PANEL), f32) for _ in range(groups)] for _ in sides]
    sides = [list(side) for side in sides]
    scales = []
    for r in range(0, WINDOW, 2):
        h, t = r // 8, r % 8
        first, second = columns[r], columns[r + 1]
        a, b, c = first[h][t : t + 1], first[h][t + 1 : t + 2], second[h][t + 1 : t + 2]
        det = a * c - b * b
        q = reciprocal(det)
        root_a = lax.rsqrt(a)
        inv_a = root_a * root_a
        root_d = lax.rsqrt(det * inv_a)
        slope = b * inv_a
        scales.append((a * q, b * q, c * q))
        l0, l1 = [], []
        pair = (row8 == t) | (row8 == t + 1)
        for g in range(groups):
            f, d = first[g], second[g]
            if g == h:
                f, d = jnp.where(pair, 0.0, f), jnp.where(pair, 0.0, d)
            l0.append((c * f - b * d) * q)
            l1.append((a * d - b * f) * q)
        for j in range(r + 2, WINDOW):
            x, y = columns[j][h][t : t + 1], columns[j][h][t + 1 : t + 2]
            columns[j] = [columns[j][g] - (l0[g] * x + l1[g] * y) for g in range(groups)]
        for n, side in enumerate(sides):
            x, y = side[h][t : t + 1], side[h][t + 1 : t + 2]
            uppers[n][h] = jnp.where(row8 == t, x * root_a, jnp.where(row8 == t + 1, (y - slope * x) * root_d, uppers[n][h]))
            sides[n] = [side[g] - (l0[g] * x + l1[g] * y) for g in range(groups)]
    solved = []
    for side in sides:
        rows = []
        for r in range(0, WINDOW, 2):
            h, t = r // 8, r % 8
            aq, bq, cq = scales[r // 2]
            x, y = side[h][t : t + 1], side[h][t + 1 : t + 2]
            rows += [cq * x - bq * y, aq * y - bq * x]
        solved.append(rows)
    return uppers, solved

def factor_steps(block, result, zero):
    lane8 = lax.broadcasted_iota(jnp.int32, (8, PANEL), 1)
    row8 = lax.broadcasted_iota(jnp.int32, (8, PANEL), 0)
    groups = PANEL // 8
    per_window = WINDOW // 8
    left = [block[8 * i : 8 * i + 8] for i in range(groups)]
    right = [(lane8 == row8 + 8 * i).astype(f32) for i in range(groups)]
    uppers, inverses = [], []
    for window in range(PANEL // WINDOW):
        k = window * WINDOW
        first = window * per_window
        mine = range(first, first + per_window)
        columns = [[jnp.broadcast_to(left[g][:, k + c : k + c + 1], (8, PANEL)) + zero if g == first else jnp.broadcast_to(left[g][:, k + c : k + c + 1], (8, PANEL)) for g in mine] for c in range(WINDOW)]
        (up_l, up_r), (w_l, w_r) = eliminate(columns, [[left[g] for g in mine], [right[g] for g in mine]])
        uppers += [jnp.where(lane8 >= row8 + 8 * g, u, 0.0) for g, u in zip(mine, up_l)]
        inverses += up_r
        near = min(groups, (k // SUPER + 1) * SUPER // 8)
        for i in range(first + per_window, near):
            scale = [jnp.broadcast_to(left[i][:, k + c : k + c + 1], (8, PANEL)) for c in range(WINDOW)]
            left[i] = left[i] - tree([scale[c] * w_l[c] for c in range(WINDOW)])
            right[i] = right[i] - tree([scale[c] * w_r[c] for c in range(WINDOW)])
        if (k + WINDOW) % SUPER == 0 and near < groups:
            parts = SUPER // 8
            up = jnp.concatenate(uppers[-parts:], 0)
            inv = jnp.concatenate(inverses[-parts:], 0)
            mult = up[:, near * 8 :]
            chg_l = transposed_dot(mult, up, highest)
            chg_r = transposed_dot(mult, inv, highest)
            for i in range(near, groups):
                o = (i - near) * 8
                left[i] = left[i] - chg_l[o : o + 8]
                right[i] = right[i] - chg_r[o : o + 8]
        if (k + WINDOW) % SUPER == 0:
            result.append((jnp.concatenate(uppers[-SUPER // 8 :], 0), jnp.concatenate(inverses[-SUPER // 8 :], 0)))
        yield

def whiten_kernel(scale, index_ref, down_ref, *refs):
    *row_refs, factor_hbm, out_hbm, hidden_ref, a_ref, u_ref, inverse_ref, out_ref, sems = refs
    width = hidden_ref.shape[1]
    step = row_refs[0].shape[0]
    for i, row_ref in enumerate(row_refs):
        hidden_ref[i * step : (i + 1) * step, :] = row_ref[...]
    blocks = width // PANEL
    steps = PANEL // WINDOW
    share = factor_hbm.shape[0]
    leaving = []
    zero = jnp.full((8, PANEL), jnp.where(index_ref[0] < 0, 1.0, 0.0), f32)

    def gram(b, lo, hi):
        s = b * PANEL
        g = transposed_dot(hidden_ref[:, s : s + PANEL], hidden_ref[:, lo:hi]) * scale
        row = lax.broadcasted_iota(jnp.int32, g.shape, 0) + s
        lane = lax.broadcasted_iota(jnp.int32, g.shape, 1) + lo
        return jnp.where(row == lane, g + damping, g)

    def chunks(start):
        return [(c, min(c + CHUNK, width)) for c in range(start, width, CHUNK)]

    def store_gram(b, lo, hi):
        a_ref[b * PANEL : (b + 1) * PANEL, lo:hi] = gram(b, lo, hi)

    def panel(p, lo, hi):
        s, e = p * PANEL, (p + 1) * PANEL
        u_ref[s:e, lo:hi] = jnp.dot(inverse_ref[p % 2], a_ref[s:e, lo:hi], preferred_element_type=f32, precision=highest)

    def trail(p, b, lo, hi):
        s, e, t = p * PANEL, (p + 1) * PANEL, b * PANEL
        a_ref[t : t + PANEL, lo:hi] = a_ref[t : t + PANEL, lo:hi] - transposed_dot(u_ref[s:e, t : t + PANEL], u_ref[s:e, lo:hi], highest)

    def output(p):
        s, e = p * PANEL, (p + 1) * PANEL
        rows = u_ref[s:e, s:]
        high = rows.astype(bf16)
        low = (rows - high.astype(f32)).astype(bf16)
        down = down_ref[s:, :]
        out_ref[s:e, :] = jnp.dot(high, down, preferred_element_type=f32) + jnp.dot(low, down, preferred_element_type=f32)
        copy = pltpu.make_async_copy(out_ref.at[s:e], out_hbm.at[s:e], sems.at[p])
        copy.start()
        leaving.append(copy)

    def clear(p):
        if p: u_ref[p * PANEL : (p + 1) * PANEL, : p * PANEL] = jnp.zeros((PANEL, p * PANEL), f32)

    block = gram(0, 0, PANEL)
    work = [functools.partial(store_gram, 0, lo, hi) for lo, hi in chunks(PANEL)]
    for b in range(1, blocks):
        work += [functools.partial(store_gram, b, lo, hi) for lo, hi in chunks(b * PANEL)]
        work.append(functools.partial(clear, b))
    def first_half(p, upper, inverse):
        s, e = p * PANEL, (p + 1) * PANEL
        m = s + SUPER
        u_ref[s:m, s:e] = upper
        if e < width:
            inverse_ref[p % 2, :SUPER] = inverse
            a_next = a_ref[s:m, e : e + PANEL]
            u_ref[s:m, e : e + PANEL] = jnp.dot(inverse[:, :SUPER], a_next, preferred_element_type=f32, precision=highest)

    def first_gram(p):
        s, e = p * PANEL, (p + 1) * PANEL
        top = u_ref[s : s + SUPER, e : e + PANEL]
        a_ref[e : e + PANEL, e : e + PANEL] = a_ref[e : e + PANEL, e : e + PANEL] - transposed_dot(top, top, highest)

    half = SUPER // WINDOW
    for p in range(blocks):
        s, e = p * PANEL, (p + 1) * PANEL
        m = s + SUPER
        result = []
        done = 0
        for i, _ in enumerate(factor_steps(block, result, zero)):
            if i == half:
                first_half(p, *result[0])
            if i == half + 1 and e < width:
                first_gram(p)
            upto = len(work) * (i + 1) // steps
            for job in work[done:upto]: job()
            done = upto
        upper, inverse = result[1]
        u_ref[m:e, s:e] = upper
        if e < width:
            inverse_ref[p % 2, SUPER:] = inverse
            low = jnp.dot(inverse, a_ref[s:e, e:e+PANEL], preferred_element_type=f32, precision=highest)
            u_ref[m:e, e:e+PANEL] = low
            block = jnp.concatenate([
                a_ref[e + o : e + o + SUPER, e : e + PANEL] - transposed_dot(low[:, o : o + SUPER], low, highest)
                for o in range(0, PANEL, SUPER)], 0)
            f = e + PANEL
            work = [functools.partial(panel, p, lo, hi) for lo, hi in chunks(f)]
            work += [functools.partial(trail, p, p + 1, lo, hi) for lo, hi in chunks(f)]
            for b in range(p + 2, blocks):
                work += [functools.partial(trail, p, b, lo, hi) for lo, hi in chunks(b * PANEL)]
            work.append(functools.partial(output, p))
    rows = pl.ds(pl.multiple_of(index_ref[0] * share, 8), share)
    copy = pltpu.make_async_copy(u_ref.at[rows], factor_hbm, sems.at[blocks])
    copy.start()
    output(blocks - 1)
    for item in leaving + [copy]:
        item.wait()


def whiten(index, rows, down, share, slot_total):
    width, columns = down.shape
    vmem = pl.BlockSpec(memory_space=pltpu.VMEM)
    return pl.pallas_call(
        functools.partial(whiten_kernel, 1.0 / slot_total),
        out_shape=(jax.ShapeDtypeStruct((share, width), f32), jax.ShapeDtypeStruct((width, columns), f32)),
        in_specs=[pl.BlockSpec(memory_space=pltpu.SMEM), vmem] + [vmem] * len(rows),
        out_specs=(pl.BlockSpec(memory_space=pl.ANY), pl.BlockSpec(memory_space=pl.ANY)),
        scratch_shapes=[
            pltpu.VMEM((len(rows) * rows[0].shape[0], width), bf16),
            pltpu.VMEM((width, width), f32),
            pltpu.VMEM((width, width), f32),
            pltpu.VMEM((2, PANEL, PANEL), f32),
            pltpu.VMEM((width, columns), f32),
            pltpu.SemaphoreType.DMA((width // PANEL + 1,)),
        ],
        compiler_params=pltpu.CompilerParams(vmem_limit_bytes=48 * 2**20),
        name="whiten",
    )(index, down, *rows)


def project_kernel(index_ref, token_ref, *refs):
    *weight_refs, send_ref, keep_ref = refs
    slots, both = keep_ref.shape
    chips = send_ref.shape[0] + 1
    width = both // 2
    depth = weight_refs[0].shape[0]
    chip, core = index_ref[0], index_ref[1]
    starts = [core * depth, (1 - core) * depth]
    for k in range(chips):
        owner = lax.rem(chip + k + 1, chips)
        rows = pl.ds(pl.multiple_of(owner * slots, 16), slots)
        for half in range(2):
            total = None
            for j in range(CORES):
                part = jnp.dot(
                    token_ref[rows, pl.ds(pl.multiple_of(starts[j], depth), depth)],
                    weight_refs[2 * j + half][...],
                    preferred_element_type=f32,
                )
                total = part if total is None else total + part
            columns = slice(half * width, (half + 1) * width)
            if k < chips - 1:
                send_ref[k, :, columns] = total * LINK_SCALE
            else:
                keep_ref[:, columns] = total


def project(index, tokens, weights, chips):
    vmem = pl.BlockSpec(memory_space=pltpu.VMEM)
    both = 2 * weights[0].shape[1]
    slots = tokens.shape[0] // chips
    return pl.pallas_call(
        project_kernel,
        out_shape=(
            jax.ShapeDtypeStruct((chips - 1, slots, both), f32),
            jax.ShapeDtypeStruct((slots, both), f32),
        ),
        in_specs=[pl.BlockSpec(memory_space=pltpu.SMEM)] + [vmem] * (1 + len(weights)),
        out_specs=(vmem, vmem),
        compiler_params=pltpu.CompilerParams(vmem_limit_bytes=48 * 2**20),
        name="project",
    )(index, tokens, *weights)


def body(tokens, expert_ids, gate_weight, up_weight, down_weight):
    experts = lax.axis_size("expert")
    owners = experts * gate_weight.shape[0]
    dp_size = lax.axis_size("dp")
    chips = dp_size // CORES
    dp = lax.axis_index("dp")
    chip, core = dp // CORES, dp % CORES
    width = gate_weight.shape[2]
    tok_rows, model = tokens.shape

    def to_chip(x, k):
        steps = [(i, (i + k * CORES) % dp_size) for i in range(dp_size)]
        return lax.ppermute(x, "dp", steps)

    def to_core(x):
        return lax.ppermute(x, "dp", [(i, i ^ 1) for i in range(dp_size)])

    gate, up = gate_weight[0], up_weight[0]
    weights = [gate, up, to_core(gate), to_core(up)]

    expert_range = jnp.arange(owners, dtype=jnp.int32)
    member = jnp.any(expert_ids[:, :, None] == expert_range[None, None, :], axis=1)
    earlier = (jnp.arange(tok_rows)[:, None] > jnp.arange(tok_rows)[None, :]).astype(jnp.int32)
    ranking = jnp.dot(earlier, member.astype(jnp.int32))
    slot_range = jnp.arange(CAP, dtype=jnp.int32)
    placing = (member[:, :, None] & (ranking[:, :, None] == slot_range[None, None, :])).astype(bf16)
    outgoing = jnp.einsum(
        "tec,tyd->yecd",
        placing,
        tokens.reshape(tok_rows, chips, model // chips),
        preferred_element_type=f32,
    ).astype(bf16)
    groups = [
        [(y * CORES + c) * experts + e for y in range(chips) for e in range(experts)]
        for c in range(CORES)
    ]
    arrived = lax.all_to_all(
        outgoing.reshape(chips * owners, CAP, model // chips),
        ("dp", "expert"),
        split_axis=0,
        concat_axis=0,
        axis_index_groups=groups,
        tiled=True,
    )
    received = arrived.reshape(-1, model // chips)
    slot_total = received.shape[0] // chips

    index = jnp.stack([chip, core]).astype(jnp.int32)
    sent, total = project(index, received, weights, chips)
    for k in range(1, chips):
        total = total + to_chip(sent[k - 1].astype(f16), k).astype(f32) * (1.0 / LINK_SCALE)
    gate_sum, up_sum = total[:, :width], total[:, width:]
    hidden = (gate_sum / (1.0 + jnp.exp(-gate_sum)) * up_sum).astype(bf16)
    rows = [hidden] + [to_chip(hidden, k) for k in range(1, chips)]
    rows = rows + [to_core(row) for row in rows]
    factor, whitened = whiten(
        dp.astype(jnp.int32)[None], rows, down_weight[0], width // dp_size, slot_total
    )
    return (factor[None], whitened[None])


def solution(mesh):
    return jax.shard_map(
        body,
        mesh=mesh,
        in_specs=(
            P(("dp", "expert"), None),
            P(("dp", "expert"), None),
            P("expert", "dp", None),
            P("expert", "dp", None),
            P("expert", None, "dp"),
        ),
        out_specs=(P("expert", "dp", None), P("expert", None, "dp")),
        check_vma=False,
    )
```
